32 devices in a mesh: layer: 2 (over y), unit: 8 (over z, x), feat: 2 (over core).
Axes of the slice: x: 2, y: 2, z: 4, core: 2. Of those that a mesh axis runs over, the one named last changes fastest.
Arguments:
- units: bfloat16 [57344, 24576], P(('layer', 'unit'), 'feat'), parts along dimension 0, may hold values from -1 to 1
- assign: int32 [57344], P(('layer', 'unit')), parts along dimension 0, may hold values from 0 to 511, as said below
- panel_idx: int32 [1024], P(('layer', 'unit')), parts along dimension 0, may hold values from 0 to 28671, as said below
Outputs:
- distances: float32 [1024, 512], P(('layer', 'unit'), 'feat'), parts along dimension 0
The draws below stay inside these ranges and needn't reach their ends.
There are 2 independent parts, one for each index of `layer`. The reference program is written for one: setup_inputs(seed, part) draws one part's arguments, and reference() takes and returns one part's arrays. A program takes and returns all parts, laid end to end along the dimension named above; each array names one. Nothing has to cross between parts.
Inputs may be any that keep to these rules, and one draw needn't show every extreme that they name: `assign`: in each aligned block of 3584 entries, at most 896 name centroids of one owner (centroid // 64), and in every block some owner is named exactly 896 times. `panel_idx`: the entries of each aligned block of 64 index units of the matching aligned block of 3584 units.
All inputs are finite; a program needn't handle non-finite values.
Results may differ from the reference program's by a relative error of at most 0.0003.
Values may be sent and summed in bfloat16 or wider, within the bound.
A program may use at most 192 MiB of HBM per device.

```python
import math
import jax
import jax.numpy as jnp
from jax import lax

F = 24576
UNITS = 28672
CENT_DEV = 64
PANEL_DEV = 64
UNIT_DEV = 3584
K = 512
PANEL = 512


shared_rank = 128


def draw_units(key, part):
    key = jax.random.fold_in(key, 1)
    key_values, key_scales, key_dirs, key_mean, key_coef = jax.random.split(key, 5)
    directions = jax.random.normal(key_dirs, (shared_rank, F), jnp.float32) * (1.0 / math.sqrt(F))
    values_drawn = jnp.clip(jax.random.normal(key_values, (UNITS, F), jnp.float32), -6.0, 6.0)
    scales = jnp.exp(jax.random.uniform(key_scales, (UNITS, 1), jnp.float32, math.log(0.5), math.log(2.0)))
    mean_coef = jax.random.normal(key_mean, (1, shared_rank), jnp.float32)
    spread_coef = jnp.clip(jax.random.normal(key_coef, (UNITS, shared_rank), jnp.float32), -6.0, 6.0)
    coefficients = mean_coef + spread_coef
    shared = jnp.dot(coefficients, directions, precision=lax.Precision.HIGHEST) * (1.0 / math.sqrt(shared_rank))
    mixed = 0.8 * shared + 0.6 * values_drawn * (1.0 / math.sqrt(F))
    return jnp.clip(mixed * scales, -1.0, 1.0).astype(jnp.bfloat16)


def draw_assign(key, part):
    key = jax.random.fold_in(key, 2)
    blocks = UNITS // UNIT_DEV
    mean_load = UNIT_DEV // blocks
    loads = jnp.full((blocks,), mean_load, jnp.int32)
    loads = loads.at[0].set(2 * mean_load).at[1].set(mean_load // 2).at[2].set(mean_load - mean_load // 2)
    bounds = jnp.cumsum(loads)
    slot_rank = jnp.sum((jnp.arange(UNIT_DEV, dtype=jnp.int32)[:, None] >= bounds[None, :]).astype(jnp.int32), axis=1)
    key_owner, key_low, key_high = jax.random.split(key, 3)

    def one_block(block_key):
        key_perm, key_slots = jax.random.split(block_key)
        owner_perm = jax.random.permutation(key_perm, blocks).astype(jnp.int32)
        slot_perm = jax.random.permutation(key_slots, UNIT_DEV).astype(jnp.int32)
        return owner_perm[slot_rank[slot_perm]]
    owner_ids = jax.vmap(one_block)(jax.random.split(key_owner, blocks)).reshape(-1)
    lower = jax.random.randint(key_low, (UNITS,), 0, CENT_DEV, jnp.int32)
    higher = jax.random.randint(key_high, (UNITS,), 0, CENT_DEV, jnp.int32)
    return (owner_ids * CENT_DEV + jnp.minimum(lower, higher)).astype(jnp.int32)


def draw_panel_idx(key, part):
    key = jax.random.fold_in(key, 3)
    offsets = jax.random.randint(key, (PANEL,), 0, UNIT_DEV, jnp.int32)
    block_ids = jnp.arange(PANEL, dtype=jnp.int32) // PANEL_DEV
    return (block_ids * UNIT_DEV + offsets).astype(jnp.int32)


def setup_inputs(seed: int = 0, part: int = 0) -> dict:
    key_list = jax.random.split(jax.random.key(seed), 4)
    own_keys = jax.random.split(jax.random.fold_in(key_list[3], part), 4)
    return {
        "units": draw_units(jax.random.fold_in(jax.random.fold_in(key_list[3], part), 71), part),
        "assign": draw_assign(jax.random.fold_in(jax.random.fold_in(key_list[3], part), 71), part),
        "panel_idx": draw_panel_idx(jax.random.fold_in(jax.random.fold_in(key_list[3], part), 71), part),
    }


def reference(units, assign, panel_idx):
    counts = jax.ops.segment_sum(jnp.ones((UNITS,), jnp.float32), assign, num_segments=K)
    cent_sums = jax.ops.segment_sum(units.astype(jnp.float32), assign, num_segments=K)
    centroids = (cent_sums / jnp.maximum(counts, 1.0)[:, None]).astype(jnp.bfloat16)
    panel_rows = jnp.take(units, panel_idx, axis=0)
    panel_float = panel_rows.astype(jnp.float32)
    panel_norms = jnp.sum(panel_float * panel_float, axis=1)
    cent_float = centroids.astype(jnp.float32)
    cent_norms = jnp.sum(cent_float * cent_float, axis=1)
    inner = jnp.dot(panel_rows, centroids.T, preferred_element_type=jnp.float32)
    return panel_norms[:, None] + cent_norms[None, :] - 2.0 * inner
```

```python
import functools

import jax
import jax.numpy as jnp
from jax import lax
from jax.experimental import pallas as pl
from jax.experimental.pallas import tpu as pltpu
from jax.sharding import PartitionSpec as P

CENT_DEV = 64
PIECE = 256
LAG = 4
MESH = pl.DeviceIdType.MESH
NT = (((1,), (1,)), ((), ()))


def group_quarter(z, g):
    inner = jnp.where(g == 0, 3, jnp.where(g == 1, 0, jnp.where(g == 2, 2, 1)))
    outer = 3 - g
    near = jnp.where((z == 0) | (z == 3), outer, inner)
    return jnp.where(z < 2, near, 3 - near)


def kernel(
    subs, panel_dev,
    assign_ref, panel_ref, units_ref, out_ref,
    member, ubuf, xsend, own, xrecv, urecv, drecv, acc, fin,
    psend, precv, hist, hrecv, gram, norm, pnorm, dhalf, frecv, esum, erecv,
    usem, xs_sem, xr_sem, zs_sem, ur_sem, dr_sem,
    ps_sem, pr_sem, hs_sem, hr_sem, f_sem, es_sem, er_sem,
):
    me = lax.axis_index("unit")
    feat = lax.axis_index("feat")
    z, x = me // 2, me % 2
    mate = me + 1 - 2 * x
    cents = own.shape[1]
    rows = units_ref.shape[0]
    pieces = 4 * subs

    barrier = pltpu.get_barrier_semaphore()
    for d in range(1, 8):
        pl.semaphore_signal(
            barrier, inc=1, device_id={"unit": (me + d) % 8}, device_id_type=MESH
        )
    pl.semaphore_signal(barrier, inc=1, device_id={"feat": 1 - feat}, device_id_type=MESH)

    def fetch(t):
        i, h = t // 2, t % 2
        q = group_quarter(z, i // subs)
        side = jnp.where(h == 0, 1 - x, x)
        start = ((side * 4 + q) * subs + i % subs) * PIECE
        return pltpu.make_async_copy(
            units_ref.at[:, pl.ds(pl.multiple_of(start, PIECE), PIECE)],
            ubuf.at[t % 3],
            usem.at[t % 3],
        )

    fetch(0).start()
    fetch(1).start()

    def build(b, carry):
        first = pl.multiple_of(b * 64, 64)
        ids = lax.broadcasted_iota(jnp.int32, (64, rows), 0) + first
        member[pl.ds(first, 64), :] = jnp.where(ids == assign_ref[...], 1.0, 0.0).astype(jnp.bfloat16)
        return carry

    lax.fori_loop(0, cents // 64, build, 0)
    unit_ids = lax.broadcasted_iota(jnp.int32, (panel_dev, rows), 1)
    member[cents : cents + panel_dev, :] = jnp.where(unit_ids == panel_ref[...], 1.0, 0.0).astype(jnp.bfloat16)

    def x_copy(i):
        return pltpu.make_async_remote_copy(
            src_ref=xsend.at[i], dst_ref=xrecv.at[i], send_sem=xs_sem.at[i], recv_sem=xr_sem.at[i],
            device_id={"unit": mate}, device_id_type=MESH,
        )

    def up_copy(i, slot):
        return pltpu.make_async_remote_copy(
            src_ref=own.at[i], dst_ref=urecv.at[slot], send_sem=zs_sem.at[i], recv_sem=ur_sem.at[slot],
            device_id={"unit": (me + 2) % 8}, device_id_type=MESH,
        )

    def down_copy(i, slot):
        return pltpu.make_async_remote_copy(
            src_ref=own.at[i], dst_ref=drecv.at[slot], send_sem=zs_sem.at[i], recv_sem=dr_sem.at[slot],
            device_id={"unit": (me + 6) % 8}, device_id_type=MESH,
        )

    def panel_copy(to, source):
        return pltpu.make_async_remote_copy(
            src_ref=psend.at[to], dst_ref=precv.at[:, pl.ds(pl.multiple_of(source * panel_dev, panel_dev), panel_dev), :],
            send_sem=ps_sem.at[to], recv_sem=pr_sem.at[source],
            device_id={"unit": to}, device_id_type=MESH,
        )

    def hist_copy(to, source):
        return pltpu.make_async_remote_copy(
            src_ref=hist, dst_ref=hrecv.at[source], send_sem=hs_sem.at[to], recv_sem=hr_sem.at[source],
            device_id={"unit": to}, device_id_type=MESH,
        )

    def sum_copy(to, source):
        return pltpu.make_async_remote_copy(
            src_ref=esum.at[pl.ds(pl.multiple_of(to * panel_dev, panel_dev), panel_dev), :], dst_ref=erecv.at[source],
            send_sem=es_sem.at[to], recv_sem=er_sem.at[source],
            device_id={"unit": to}, device_id_type=MESH,
        )

    pl.semaphore_wait(barrier, 8)

    def compute(t, carry):
        i, h = t // 2, t % 2
        q, s = group_quarter(z, i // subs), i % subs
        side = jnp.where(h == 0, 1 - x, x)
        to = 2 * q + side

        @pl.when(t + 2 < 2 * pieces)
        def _():
            fetch(t + 2).start()

        fetch(t).wait()
        part = jnp.dot(member[...], ubuf[t % 3], preferred_element_type=jnp.float32).astype(jnp.bfloat16)

        @pl.when(h == 0)
        def _():
            xsend[i] = part[:cents]
            x_copy(i).start()

        @pl.when(h == 1)
        def _():
            own[i] = part[:cents]

        @pl.when(to == me)
        def _():
            precv[s, pl.ds(pl.multiple_of(me * panel_dev, panel_dev), panel_dev), :] = part[cents:]

        @pl.when(to != me)
        def _():
            psend[to, s] = part[cents:]

            @pl.when(s == subs - 1)
            def _():
                panel_copy(to, me).start()

        return carry

    def reduce(i):
        q, s = group_quarter(z, i // subs), i % subs
        slot = q * subs + s
        x_copy(i).wait_recv()
        acc[...] = own[i].astype(jnp.float32) + xrecv[i].astype(jnp.float32)

        @pl.when((z > 0) & (q >= z))
        def _():
            up_copy(i, slot).wait_recv()
            acc[...] += urecv[slot].astype(jnp.float32)

        @pl.when((z < 3) & (q <= z))
        def _():
            down_copy(i, slot).wait_recv()
            acc[...] += drecv[slot].astype(jnp.float32)

        @pl.when(q > z)
        def _():
            own[i] = acc[...].astype(jnp.bfloat16)
            up_copy(i, slot).start()

        @pl.when(q < z)
        def _():
            own[i] = acc[...].astype(jnp.bfloat16)
            down_copy(i, slot).start()

        @pl.when(q == z)
        def _():
            fin[s] = acc[...].astype(jnp.bfloat16)

    def step(i, carry):
        @pl.when(i < pieces)
        def _():
            lax.fori_loop(2 * i, 2 * i + 2, compute, 0)

        @pl.when(i == 2)
        def _():
            ones = jnp.ones((8, rows), jnp.bfloat16)
            hist[...] = lax.dot_general(ones, member[:cents, :], NT, preferred_element_type=jnp.float32)
            hrecv[me] = hist[...]
            for d in range(1, 8):
                hist_copy((me + d) % 8, me).start()

        @pl.when(i >= LAG)
        def _():
            reduce(i - LAG)

        return carry

    lax.fori_loop(0, pieces + LAG, step, 0)

    for d in range(1, 8):
        source = (me + d) % 8
        hist_copy(source, source).wait_recv()
        panel_copy(source, source).wait_recv()

    gram[...] = jnp.zeros_like(gram)
    norm[...] = jnp.zeros_like(norm)
    pnorm[...] = jnp.zeros_like(pnorm)

    def finish(s, carry):
        panel, cent = precv[s], fin[s]
        gram[...] += lax.dot_general(panel, cent, NT, preferred_element_type=jnp.float32)
        wide = cent.astype(jnp.float32)
        square = wide * wide
        high = square.astype(jnp.bfloat16)
        low = (square - high.astype(jnp.float32)).astype(jnp.bfloat16)
        ones = jnp.ones((8, PIECE), jnp.bfloat16)
        norm[...] += lax.dot_general(ones, high, NT, preferred_element_type=jnp.float32)
        norm[...] += lax.dot_general(ones, low, NT, preferred_element_type=jnp.float32)
        panel_wide = panel.astype(jnp.float32)
        panel_square = panel_wide * panel_wide
        pnorm[...] += panel_square[:, :128] + panel_square[:, 128:]
        return carry

    lax.fori_loop(0, subs, finish, 0)

    counts = hrecv[0][0:1, :]
    for v in range(1, 8):
        counts = counts + hrecv[v][0:1, :]
    inverse = 1.0 / jnp.maximum(counts, 1.0)
    cent_norm = norm[0:1, :] * inverse * inverse
    panel_norm = jnp.sum(pnorm[...], axis=1, keepdims=True)
    half = cents // 2
    for h in range(2):
        lanes = slice(h * half, (h + 1) * half)
        dhalf[h] = panel_norm + cent_norm[:, lanes] - 2.0 * (gram[:, lanes] * inverse[:, lanes])
    swap = pltpu.make_async_remote_copy(
        src_ref=dhalf.at[1 - feat], dst_ref=frecv, send_sem=f_sem.at[0], recv_sem=f_sem.at[1],
        device_id={"feat": 1 - feat}, device_id_type=MESH,
    )
    swap.start()
    swap.wait_recv()
    esum[...] = dhalf[feat] + frecv[...]
    for d in range(1, 8):
        sum_copy((me + d) % 8, me).start()
    erecv[me] = esum[pl.ds(pl.multiple_of(me * panel_dev, panel_dev), panel_dev), :]
    for d in range(1, 8):
        source = (me + d) % 8
        sum_copy(source, source).wait_recv()
    total = erecv[0]
    for v in range(1, 8):
        total = total + erecv[v]
    out_ref[...] = total

    swap.wait_send()
    for d in range(1, 8):
        to = (me + d) % 8
        hist_copy(to, me).wait_send()
        panel_copy(to, me).wait_send()
        sum_copy(to, me).wait_send()

    def drain(i, carry):
        x_copy(i).wait_send()
        q = group_quarter(z, i // subs)

        @pl.when(q > z)
        def _():
            up_copy(i, q * subs + i % subs).wait_send()

        @pl.when(q < z)
        def _():
            down_copy(i, q * subs + i % subs).wait_send()

        return carry

    lax.fori_loop(0, pieces, drain, 0)


def fused_shards(units, assign, panel_idx):
    rows, features = units.shape
    panel_dev = panel_idx.shape[0]
    cents = CENT_DEV * 8
    subs = features // (8 * PIECE)
    pieces = 4 * subs
    local_rows = panel_idx - lax.axis_index("unit") * rows
    bf16, f32, dma = jnp.bfloat16, jnp.float32, pltpu.SemaphoreType.DMA
    panel = 8 * panel_dev
    half = cents // 2
    block = pltpu.VMEM((pieces, cents, PIECE), bf16)
    vmem = pl.BlockSpec(memory_space=pltpu.VMEM)
    return pl.pallas_call(
        functools.partial(kernel, subs, panel_dev),
        out_shape=jax.ShapeDtypeStruct((panel_dev, half), f32),
        in_specs=[vmem, vmem, pl.BlockSpec(memory_space=pl.ANY)],
        out_specs=vmem,
        scratch_shapes=[
            pltpu.VMEM((cents + panel_dev, rows), bf16),
            pltpu.VMEM((3, rows, PIECE), bf16),
            block, block, block, block, block,
            pltpu.VMEM((cents, PIECE), f32),
            pltpu.VMEM((subs, cents, PIECE), bf16),
            pltpu.VMEM((8, subs, panel_dev, PIECE), bf16),
            pltpu.VMEM((subs, panel, PIECE), bf16),
            pltpu.VMEM((8, cents), f32),
            pltpu.VMEM((8, 8, cents), f32),
            pltpu.VMEM((panel, cents), f32),
            pltpu.VMEM((8, cents), f32),
            pltpu.VMEM((panel, 128), f32),
            pltpu.VMEM((2, panel, half), f32),
            pltpu.VMEM((panel, half), f32),
            pltpu.VMEM((panel, half), f32),
            pltpu.VMEM((8, panel_dev, half), f32),
            dma((3,)), dma((pieces,)), dma((pieces,)), dma((pieces,)), dma((pieces,)), dma((pieces,)),
            dma((8,)), dma((8,)), dma((8,)), dma((8,)), dma((2,)), dma((8,)), dma((8,)),
        ],
        cost_estimate=pl.CostEstimate(
            flops=2 * (cents + panel_dev) * rows * features,
            bytes_accessed=2 * rows * features,
            transcendentals=0,
        ),
        compiler_params=pltpu.CompilerParams(
            collective_id=0, has_side_effects=True, vmem_limit_bytes=60 * 1024 * 1024
        ),
    )(assign.reshape(1, rows), local_rows.reshape(panel_dev, 1), units)


def shards(units, assign, panel_idx):
    unit_rows = units.shape[0]
    owners = lax.axis_size("unit")
    cent_dev = CENT_DEV
    all_cents = cent_dev * owners
    my_index = lax.axis_index("unit")
    cent_ids = lax.iota(jnp.int32, cent_dev * lax.axis_size("unit"))
    member = (cent_ids[:, None] == assign[None, :]).astype(jnp.bfloat16)
    cent_sums = lax.psum_scatter(
        jnp.dot(member, units, preferred_element_type=jnp.float32).astype(jnp.bfloat16),
        "unit",
        scatter_dimension=0,
        tiled=True,
    ).astype(jnp.float32)
    histogram = jnp.sum(
        (assign[:, None] == lax.iota(jnp.int32, all_cents)[None, :]).astype(jnp.float32), axis=0
    )
    totals = lax.psum(histogram, "unit")
    counts = lax.dynamic_slice_in_dim(totals, my_index * cent_dev, cent_dev)
    centroids = (cent_sums / jnp.maximum(counts, 1.0)[:, None]).astype(jnp.bfloat16)
    local_rows = panel_idx - my_index * unit_rows
    panel_rows = jnp.take(units, local_rows, axis=0)
    panel_float = panel_rows.astype(jnp.float32)
    panel_norms = jnp.sum(panel_float * panel_float, axis=1)
    pieces = lax.all_gather(centroids, "unit", axis=0, tiled=True)
    cent_float = pieces.astype(jnp.float32)
    cent_norms = jnp.sum(cent_float * cent_float, axis=1)
    inner_block = lax.dot_general(
        panel_rows, pieces, (((1,), (1,)), ((), ())), preferred_element_type=jnp.float32
    )
    block_terms = panel_norms[:, None] + cent_norms[None, :] - 2.0 * inner_block
    return lax.psum_scatter(block_terms, "feat", scatter_dimension=1, tiled=True)


def solution(mesh):
    in_specs = (P(("layer", "unit"), "feat"), P(("layer", "unit")), P(("layer", "unit")))
    out_specs = P(("layer", "unit"), "feat")
    fused = mesh.shape["unit"] == 8 and mesh.shape["feat"] == 2
    body = fused_shards if fused else shards
    return jax.shard_map(body, mesh=mesh, in_specs=in_specs, out_specs=out_specs, check_vma=False)
```

```python
import functools

import jax
import jax.numpy as jnp
from jax import lax
from jax.experimental import pallas as pl
from jax.experimental.pallas import tpu as pltpu
from jax.sharding import PartitionSpec as P

CENT_DEV = 64
PIECE = 256
LAG = 12
END_LAG = 8
MESH = pl.DeviceIdType.MESH
NT = (((1,), (1,)), ((), ()))


def group_quarter(z, g):
    inner = jnp.where(g == 0, 3, jnp.where(g == 1, 0, jnp.where(g == 2, 2, 1)))
    outer = 3 - g
    near = jnp.where((z == 0) | (z == 3), outer, inner)
    return jnp.where(z < 2, near, 3 - near)


def z_first(q, s):
    return (s == 1) & ((q == 0) | (q == 3))


def kernel(
    subs, panel_dev,
    assign_ref, panel_ref, units_ref, out_ref,
    member, ubuf, xsend, own, xrecv, urecv, drecv, acc, macc, murecv, mdrecv,
    psend, precv, hist, hrecv, gram, norm, pnorm, dhalf, frecv, esum, erecv,
    usem, xs_sem, xr_sem, zs_sem, ur_sem, dr_sem, ms_sem, mu_sem, md_sem,
    ps_sem, pr_sem, hs_sem, hr_sem, fs_sem, fr_sem, es_sem, er_sem,
):
    me = lax.axis_index("unit")
    feat = lax.axis_index("feat")
    z, x = me // 2, me % 2
    mate = me + 1 - 2 * x
    cents = own.shape[1]
    rows = units_ref.shape[0]
    pieces = 4 * subs
    lag = jnp.where((z == 0) | (z == 3), END_LAG, LAG)

    barrier = pltpu.get_barrier_semaphore()
    for d in range(1, 8):
        pl.semaphore_signal(
            barrier, inc=1, device_id={"unit": (me + d) % 8}, device_id_type=MESH
        )
    pl.semaphore_signal(barrier, inc=1, device_id={"feat": 1 - feat}, device_id_type=MESH)

    def fetch(t):
        i, h = t // 2, t % 2
        q = group_quarter(z, i // subs)
        side = jnp.where(h == 0, 1 - x, x)
        start = ((side * 4 + q) * subs + i % subs) * PIECE
        return pltpu.make_async_copy(
            units_ref.at[:, pl.ds(pl.multiple_of(start, PIECE), PIECE)],
            ubuf.at[t % 3],
            usem.at[t % 3],
        )

    fetch(0).start()
    fetch(1).start()

    def build(b, carry):
        first = pl.multiple_of(b * 64, 64)
        ids = lax.broadcasted_iota(jnp.int32, (64, rows), 0) + first
        member[pl.ds(first, 64), :] = jnp.where(ids == assign_ref[...], 1.0, 0.0).astype(jnp.bfloat16)
        return carry

    lax.fori_loop(0, cents // 64, build, 0)
    unit_ids = lax.broadcasted_iota(jnp.int32, (panel_dev, rows), 1)
    member[cents : cents + panel_dev, :] = jnp.where(unit_ids == panel_ref[...], 1.0, 0.0).astype(jnp.bfloat16)

    def x_copy(i):
        return pltpu.make_async_remote_copy(
            src_ref=xsend.at[i], dst_ref=xrecv.at[i], send_sem=xs_sem.at[i], recv_sem=xr_sem.at[i],
            device_id={"unit": mate}, device_id_type=MESH,
        )

    def up_copy(i, slot):
        return pltpu.make_async_remote_copy(
            src_ref=own.at[i], dst_ref=urecv.at[slot], send_sem=zs_sem.at[i], recv_sem=ur_sem.at[slot],
            device_id={"unit": (me + 2) % 8}, device_id_type=MESH,
        )

    def down_copy(i, slot):
        return pltpu.make_async_remote_copy(
            src_ref=own.at[i], dst_ref=drecv.at[slot], send_sem=zs_sem.at[i], recv_sem=dr_sem.at[slot],
            device_id={"unit": (me + 6) % 8}, device_id_type=MESH,
        )

    def mate_up_copy(i, q):
        return pltpu.make_async_remote_copy(
            src_ref=xsend.at[i], dst_ref=murecv.at[q], send_sem=ms_sem.at[q], recv_sem=mu_sem.at[q],
            device_id={"unit": (me + 2) % 8}, device_id_type=MESH,
        )

    def mate_down_copy(i, q):
        return pltpu.make_async_remote_copy(
            src_ref=xsend.at[i], dst_ref=mdrecv.at[q], send_sem=ms_sem.at[q], recv_sem=md_sem.at[q],
            device_id={"unit": (me + 6) % 8}, device_id_type=MESH,
        )

    def panel_copy(to, source, s):
        return pltpu.make_async_remote_copy(
            src_ref=psend.at[to, s],
            dst_ref=precv.at[s, pl.ds(pl.multiple_of(source * panel_dev, panel_dev), panel_dev), :],
            send_sem=ps_sem.at[to * subs + s], recv_sem=pr_sem.at[source * subs + s],
            device_id={"unit": to}, device_id_type=MESH,
        )

    def hist_copy(to, source):
        return pltpu.make_async_remote_copy(
            src_ref=hist, dst_ref=hrecv.at[source], send_sem=hs_sem.at[to], recv_sem=hr_sem.at[source],
            device_id={"unit": to}, device_id_type=MESH,
        )

    def sum_copy(to, source):
        return pltpu.make_async_remote_copy(
            src_ref=esum.at[pl.ds(pl.multiple_of(to * panel_dev, panel_dev), panel_dev), :], dst_ref=erecv.at[source],
            send_sem=es_sem.at[to], recv_sem=er_sem.at[source],
            device_id={"unit": to}, device_id_type=MESH,
        )

    gram[...] = jnp.zeros_like(gram)
    norm[...] = jnp.zeros_like(norm)
    pnorm[...] = jnp.zeros_like(pnorm)

    pl.semaphore_wait(barrier, 8)

    def compute(t, carry):
        i, h = t // 2, t % 2
        q, s = group_quarter(z, i // subs), i % subs
        side = jnp.where(h == 0, 1 - x, x)
        to = 2 * q + side

        @pl.when(t + 2 < 2 * pieces)
        def _():
            fetch(t + 2).start()

        fetch(t).wait()
        part = jnp.dot(member[...], ubuf[t % 3], preferred_element_type=jnp.float32).astype(jnp.bfloat16)

        @pl.when(h == 0)
        def _():
            xsend[i] = part[:cents]

            @pl.when(jnp.logical_not(z_first(q, s)))
            def _():
                x_copy(i).start()

        @pl.when(h == 1)
        def _():
            own[i] = part[:cents]

        @pl.when(to == me)
        def _():
            precv[s, pl.ds(pl.multiple_of(me * panel_dev, panel_dev), panel_dev), :] = part[cents:]

        @pl.when(to != me)
        def _():
            psend[to, s] = part[cents:]
            panel_copy(to, me, s).start()

        return carry

    def finish(s):
        for d in range(1, 8):
            source = (me + d) % 8
            panel_copy(source, source, s).wait_recv()
        panel, cent = precv[s], acc[...].astype(jnp.bfloat16)
        gram[...] += lax.dot_general(panel, cent, NT, preferred_element_type=jnp.float32)
        wide = cent.astype(jnp.float32)
        square = wide * wide
        high = square.astype(jnp.bfloat16)
        low = (square - high.astype(jnp.float32)).astype(jnp.bfloat16)
        ones = jnp.ones((8, PIECE), jnp.bfloat16)
        norm[...] += lax.dot_general(ones, high, NT, preferred_element_type=jnp.float32)
        norm[...] += lax.dot_general(ones, low, NT, preferred_element_type=jnp.float32)
        panel_wide = panel.astype(jnp.float32)
        panel_square = panel_wide * panel_wide
        pnorm[...] += panel_square[:, :128] + panel_square[:, 128:]

    def reduce(i):
        q, s = group_quarter(z, i // subs), i % subs
        slot = q * subs + s
        early = z_first(q, s)
        acc[...] = own[i].astype(jnp.float32)

        @pl.when(early)
        def _():
            macc[...] = xsend[i].astype(jnp.float32)

        @pl.when(jnp.logical_not(early))
        def _():
            x_copy(i).wait_recv()
            acc[...] += xrecv[i].astype(jnp.float32)

        @pl.when((z > 0) & (q >= z))
        def _():
            up_copy(i, slot).wait_recv()
            acc[...] += urecv[slot].astype(jnp.float32)

            @pl.when(early)
            def _():
                mate_up_copy(i, q).wait_recv()
                macc[...] += murecv[q].astype(jnp.float32)

        @pl.when((z < 3) & (q <= z))
        def _():
            down_copy(i, slot).wait_recv()
            acc[...] += drecv[slot].astype(jnp.float32)

            @pl.when(early)
            def _():
                mate_down_copy(i, q).wait_recv()
                macc[...] += mdrecv[q].astype(jnp.float32)

        @pl.when(early)
        def _():
            xsend[i] = macc[...].astype(jnp.bfloat16)

        @pl.when(early | (q != z))
        def _():
            own[i] = acc[...].astype(jnp.bfloat16)

        @pl.when(q > z)
        def _():
            up_copy(i, slot).start()

            @pl.when(early)
            def _():
                mate_up_copy(i, q).start()

        @pl.when(q < z)
        def _():
            down_copy(i, slot).start()

            @pl.when(early)
            def _():
                mate_down_copy(i, q).start()

        @pl.when((q == z) & early)
        def _():
            x_copy(i).start()

        @pl.when((q == z) & jnp.logical_not(early))
        def _():
            finish(s)

    def step(i, carry):
        @pl.when(i < pieces)
        def _():
            lax.fori_loop(2 * i, 2 * i + 2, compute, 0)

        @pl.when(i == 2)
        def _():
            ones = jnp.ones((8, rows), jnp.bfloat16)
            hist[...] = lax.dot_general(ones, member[:cents, :], NT, preferred_element_type=jnp.float32)
            hrecv[me] = hist[...]
            for d in range(1, 8):
                hist_copy((me + d) % 8, me).start()

        @pl.when((i >= lag) & (i < pieces + lag))
        def _():
            reduce(i - lag)

        return carry

    lax.fori_loop(0, pieces + LAG, step, 0)

    @pl.when(z_first(z, 1))
    def _():
        last = 3 * subs + 1
        x_copy(last).wait_recv()
        acc[...] = own[last].astype(jnp.float32) + xrecv[last].astype(jnp.float32)
        finish(1)

    for d in range(1, 8):
        source = (me + d) % 8
        hist_copy(source, source).wait_recv()

    counts = hrecv[0][0:1, :]
    for v in range(1, 8):
        counts = counts + hrecv[v][0:1, :]
    inverse = 1.0 / jnp.maximum(counts, 1.0)
    cent_norm = norm[0:1, :] * inverse * inverse
    panel_norm = jnp.sum(pnorm[...], axis=1, keepdims=True)
    half = cents // 2
    for h in range(2):
        lanes = slice(h * half, (h + 1) * half)
        dhalf[h] = panel_norm + cent_norm[:, lanes] - 2.0 * (gram[:, lanes] * inverse[:, lanes])
    def swap_copy(v):
        lines = pl.ds(pl.multiple_of(v * panel_dev, panel_dev), panel_dev)
        return pltpu.make_async_remote_copy(
            src_ref=dhalf.at[1 - feat, lines, :], dst_ref=frecv.at[lines, :],
            send_sem=fs_sem.at[v], recv_sem=fr_sem.at[v],
            device_id={"feat": 1 - feat}, device_id_type=MESH,
        )

    for d in range(1, 9):
        swap_copy((me + d) % 8).start()
    for d in range(1, 9):
        to = (me + d) % 8
        lines = pl.ds(pl.multiple_of(to * panel_dev, panel_dev), panel_dev)
        swap_copy(to).wait_recv()
        if d < 8:
            esum[lines, :] = dhalf[feat, lines, :] + frecv[lines, :]
            sum_copy(to, me).start()
        else:
            erecv[me] = dhalf[feat, lines, :] + frecv[lines, :]
    for d in range(1, 8):
        source = (me + d) % 8
        sum_copy(source, source).wait_recv()
    total = erecv[0]
    for v in range(1, 8):
        total = total + erecv[v]
    out_ref[...] = total

    for v in range(8):
        swap_copy(v).wait_send()
    for d in range(1, 8):
        to = (me + d) % 8
        hist_copy(to, me).wait_send()
        for s in range(subs):
            panel_copy(to, me, s).wait_send()
        sum_copy(to, me).wait_send()

    def drain(i, carry):
        q, s = group_quarter(z, i // subs), i % subs
        early = z_first(q, s)

        @pl.when(jnp.logical_not(early) | (q == z))
        def _():
            x_copy(i).wait_send()

        @pl.when(q > z)
        def _():
            up_copy(i, q * subs + s).wait_send()

            @pl.when(early)
            def _():
                mate_up_copy(i, q).wait_send()

        @pl.when(q < z)
        def _():
            down_copy(i, q * subs + s).wait_send()

            @pl.when(early)
            def _():
                mate_down_copy(i, q).wait_send()

        return carry

    lax.fori_loop(0, pieces, drain, 0)


def fused_shards(units, assign, panel_idx):
    rows, features = units.shape
    panel_dev = panel_idx.shape[0]
    cents = CENT_DEV * 8
    subs = features // (8 * PIECE)
    pieces = 4 * subs
    local_rows = panel_idx - lax.axis_index("unit") * rows
    bf16, f32, dma = jnp.bfloat16, jnp.float32, pltpu.SemaphoreType.DMA
    panel = 8 * panel_dev
    half = cents // 2
    block = pltpu.VMEM((pieces, cents, PIECE), bf16)
    vmem = pl.BlockSpec(memory_space=pltpu.VMEM)
    return pl.pallas_call(
        functools.partial(kernel, subs, panel_dev),
        out_shape=jax.ShapeDtypeStruct((panel_dev, half), f32),
        in_specs=[vmem, vmem, pl.BlockSpec(memory_space=pl.ANY)],
        out_specs=vmem,
        scratch_shapes=[
            pltpu.VMEM((cents + panel_dev, rows), bf16),
            pltpu.VMEM((3, rows, PIECE), bf16),
            block, block, block, block, block,
            pltpu.VMEM((cents, PIECE), f32), pltpu.VMEM((cents, PIECE), f32),
            pltpu.VMEM((4, cents, PIECE), bf16), pltpu.VMEM((4, cents, PIECE), bf16),
            pltpu.VMEM((8, subs, panel_dev, PIECE), bf16),
            pltpu.VMEM((subs, panel, PIECE), bf16),
            pltpu.VMEM((8, cents), f32),
            pltpu.VMEM((8, 8, cents), f32),
            pltpu.VMEM((panel, cents), f32),
            pltpu.VMEM((8, cents), f32),
            pltpu.VMEM((panel, 128), f32),
            pltpu.VMEM((2, panel, half), f32),
            pltpu.VMEM((panel, half), f32),
            pltpu.VMEM((panel, half), f32),
            pltpu.VMEM((8, panel_dev, half), f32),
            dma((3,)), dma((pieces,)), dma((pieces,)), dma((pieces,)), dma((pieces,)), dma((pieces,)),
            dma((4,)), dma((4,)), dma((4,)),
            dma((8 * subs,)), dma((8 * subs,)), dma((8,)), dma((8,)), dma((8,)), dma((8,)), dma((8,)), dma((8,)),
        ],
        cost_estimate=pl.CostEstimate(
            flops=2 * (cents + panel_dev) * rows * features,
            bytes_accessed=2 * rows * features,
            transcendentals=0,
        ),
        compiler_params=pltpu.CompilerParams(
            collective_id=0, has_side_effects=True, vmem_limit_bytes=60 * 1024 * 1024
        ),
    )(assign.reshape(1, rows), local_rows.reshape(panel_dev, 1), units)


def shards(units, assign, panel_idx):
    unit_rows = units.shape[0]
    owners = lax.axis_size("unit")
    cent_dev = CENT_DEV
    all_cents = cent_dev * owners
    my_index = lax.axis_index("unit")
    cent_ids = lax.iota(jnp.int32, cent_dev * lax.axis_size("unit"))
    member = (cent_ids[:, None] == assign[None, :]).astype(jnp.bfloat16)
    cent_sums = lax.psum_scatter(
        jnp.dot(member, units, preferred_element_type=jnp.float32).astype(jnp.bfloat16),
        "unit",
        scatter_dimension=0,
        tiled=True,
    ).astype(jnp.float32)
    histogram = jnp.sum(
        (assign[:, None] == lax.iota(jnp.int32, all_cents)[None, :]).astype(jnp.float32), axis=0
    )
    totals = lax.psum(histogram, "unit")
    counts = lax.dynamic_slice_in_dim(totals, my_index * cent_dev, cent_dev)
    centroids = (cent_sums / jnp.maximum(counts, 1.0)[:, None]).astype(jnp.bfloat16)
    local_rows = panel_idx - my_index * unit_rows
    panel_rows = jnp.take(units, local_rows, axis=0)
    panel_float = panel_rows.astype(jnp.float32)
    panel_norms = jnp.sum(panel_float * panel_float, axis=1)
    pieces = lax.all_gather(centroids, "unit", axis=0, tiled=True)
    cent_float = pieces.astype(jnp.float32)
    cent_norms = jnp.sum(cent_float * cent_float, axis=1)
    inner_block = lax.dot_general(
        panel_rows, pieces, (((1,), (1,)), ((), ())), preferred_element_type=jnp.float32
    )
    block_terms = panel_norms[:, None] + cent_norms[None, :] - 2.0 * inner_block
    return lax.psum_scatter(block_terms, "feat", scatter_dimension=1, tiled=True)


def solution(mesh):
    in_specs = (P(("layer", "unit"), "feat"), P(("layer", "unit")), P(("layer", "unit")))
    out_specs = P(("layer", "unit"), "feat")
    fused = mesh.shape["unit"] == 8 and mesh.shape["feat"] == 2
    body = fused_shards if fused else shards
    return jax.shard_map(body, mesh=mesh, in_specs=in_specs, out_specs=out_specs, check_vma=False)
```
